256 devices in a mesh: role: 2 (over y_hi), pipe: 16 (over y_lo, x, core), tp: 8 (over z).
Axes of the slice: x: 4, y: 4 (y_hi: 2, y_lo: 2; y = y_hi * 2 + y_lo), z: 8, core: 2. Of those that a mesh axis runs over, the one named last changes fastest.
Arguments:
- hidden: bfloat16 [2, 4096, 8192], P('role', 'pipe', 'tp'), may hold values from -256 to 256
- norm_gain: float32 [8192], P('tp'), may hold values from 0.1 to 1.9
- kv_weight: bfloat16 [8192, 2048], P('tp'), may hold values from -0.0625 to 0.0625
- queries: bfloat16 [2, 4096, 8192], P('role', 'pipe', 'tp'), may hold values from -128 to 128
- kv_cache: bfloat16 [2, 65536, 2048], P('role', 'pipe', 'tp'), may hold values from -5 to 5
- cache_len: int32 [2, 4096], P('role', 'pipe'), may hold values from 2 to 4096, as said below
- block_table: int32 [4352], P('pipe'), may hold values from 0 to 15, as said below
Outputs:
- attention: bfloat16 [2, 4096, 8192], P('role', 'pipe', 'tp')
- received: bfloat16 [2, 139264, 2048], P('role', 'pipe', 'tp')
The draws below stay inside these ranges and needn't reach their ends.
Inputs may be any that keep to these rules, and one draw needn't show every extreme that they name: `block_table`: entry p * 272 + b names the decode owner (a pipe index) of block b of prefill owner p. No prefill owner sends more than 34 blocks to one decode owner, and in every draw one decode owner receives exactly 34 blocks from every prefill owner. `cache_len`: in pool 0 all 256 rows of one pipe index hold the same value, that prefill owner's span offset; in pool 1 each row holds its own cached length. The value 4096 occurs in both pools of every draw.
All inputs are finite; a program needn't handle non-finite values.
Results may differ from the reference program's by a relative error of at most 0.025.
Values may be sent and summed in bfloat16 or wider, within the bound.
No kernel may reach another device: no remote copies, remote signals or barrier semaphores. Data moves between devices by JAX's collectives and lax.ppermute only.
A program may use at most 64 MiB of HBM per device.

```python
import jax
import jax.numpy as jnp
from jax import lax

D = 8192
QH = 64
KVH = 8
HD = 128
ROWS = 256
CAP = 4096
BLK = 16
NBLK = 272
CAPB = 34
N_PIPE = 16
N_TP = 8


def key_table(key):
    return jnp.clip(jax.random.normal(key, (2, N_PIPE, CAP, KVH, 2, HD), jnp.float32), -4.5, 4.5)


def draw_kv_cache(key, part):
    shared = key_table(key)
    return shared.reshape(2, N_PIPE * CAP, KVH * 2 * HD).astype(jnp.bfloat16)


def draw_queries(key, part):
    key = jax.random.fold_in(key, 12)
    group_size = QH // KVH
    drawn = 2.5 * jnp.clip(jax.random.normal(key, (2, N_PIPE, ROWS, KVH, group_size, HD), jnp.float32), -4.5, 4.5)
    return drawn.reshape(2, N_PIPE * ROWS, QH * HD).astype(jnp.bfloat16)


def draw_hidden(key, part):
    key = jax.random.fold_in(key, 13)
    column_keys = jax.random.split(key, 3)
    rising = 3.0 ** (jnp.arange(D, dtype=jnp.float32) / D)
    spread = 10.0 ** jax.random.uniform(column_keys[0], (D,), jnp.float32)
    values = jnp.clip(jax.random.normal(column_keys[2], (2, N_PIPE * ROWS, D), jnp.float32), -4.0, 4.0) * spread * rising
    return values.astype(jnp.bfloat16)


def draw_cache_len(key, part):
    key = jax.random.fold_in(key, 14)
    pieces = jax.random.split(key, 4)
    prefix = jax.random.randint(pieces[0], (N_PIPE,), 2, CAP + 1)
    prefix = prefix.at[jax.random.randint(pieces[1], (), 0, N_PIPE)].set(CAP)
    prompt_token_rows = jnp.repeat(prefix, ROWS)
    decode_rows = jax.random.randint(pieces[2], (N_PIPE * ROWS,), 2, CAP + 1)
    decode_rows = decode_rows.at[jax.random.randint(pieces[3], (), 0, N_PIPE * ROWS)].set(CAP)
    return jnp.stack([prompt_token_rows, decode_rows]).astype(jnp.int32)


def draw_block_table(key, part):
    key = jax.random.fold_in(key, 15)
    hot_owner = jax.random.randint(jax.random.fold_in(key, 1), (), 0, N_PIPE)
    candidates = jnp.arange(N_PIPE * CAPB, dtype=jnp.int32) // CAPB

    def one_source(source_key):
        order_key, shuffle_key = jax.random.split(source_key)
        ranking = jax.random.permutation(order_key, N_PIPE * CAPB).astype(jnp.int32)
        ranking = jnp.where(candidates == hot_owner, ranking - 2 * N_PIPE * CAPB, ranking)
        chosen = candidates[jnp.argsort(ranking, stable=True)[:NBLK]]
        return jax.random.permutation(shuffle_key, chosen)
    tables = jax.vmap(one_source)(jax.random.split(jax.random.fold_in(key, 2), N_PIPE))
    return tables.reshape(N_PIPE * NBLK).astype(jnp.int32)


def steps_of(key, shape, cuts, least, top_value):
    factor_of, own = 1.0, jax.random.fold_in(key, 6)
    for dim, parts in cuts:
        steps = jnp.exp(jax.random.uniform(jax.random.fold_in(own, dim), (parts,), jnp.float32, least / len(cuts), top_value / len(cuts)))
        factor_of = factor_of * jnp.repeat(steps, shape[dim] // parts).reshape([-1 if axis == dim else 1 for axis in range(len(shape))])
    return factor_of


def gaussian(stream_key, dims, scale, reach, cuts=(), kind=jnp.bfloat16):
    entries = jax.random.normal(stream_key, dims, jnp.float32) * scale
    if len(cuts) > 0:
        entries = steps_of(stream_key, dims, cuts, -0.22, 0.18) * entries
    return jnp.clip(entries, min=-reach, max=reach).astype(kind)


def setup_inputs(seed: int = 0) -> dict:
    seeds = jax.random.split(jax.random.key(seed), 8)
    return {
        "hidden": draw_hidden(jax.random.fold_in(seeds[7], 71), 0),
        "norm_gain": jnp.clip(1.0 + 0.18 * jax.random.normal(seeds[1], (D,), jnp.float32), 0.1, 1.9),
        "kv_weight": gaussian(seeds[2], (D, KVH * 2 * HD), D ** -0.5, 0.0625, ((0, 8),)),
        "queries": draw_queries(jax.random.fold_in(seeds[7], 71), 0),
        "kv_cache": draw_kv_cache(jax.random.fold_in(seeds[7], 71), 0),
        "cache_len": draw_cache_len(jax.random.fold_in(seeds[7], 71), 0),
        "block_table": draw_block_table(jax.random.fold_in(seeds[7], 71), 0),
    }


ROPE_BASE = 500000.0
EPSILON = 1e-05
NEG_FILL = -1e+30

def rotate_keys(key_rows, positions):
    rotary_half_width = key_rows.shape[-1] // 2
    frequency = ROPE_BASE ** (-2.0 * jnp.arange(rotary_half_width, dtype=jnp.float32) / key_rows.shape[-1])
    angles = positions.astype(jnp.float32)[:, None] * frequency[None, :]
    cosine = jnp.cos(angles)[:, None, :]
    sine_part = jnp.sin(angles)[:, None, :]
    front_half = key_rows[..., :rotary_half_width]
    back_half = key_rows[..., rotary_half_width:]
    return jnp.concatenate([front_half * cosine - back_half * sine_part, back_half * cosine + front_half * sine_part], axis=-1)

def project_block(hidden_rows, norm_gain, kv_weight, positions):
    features = hidden_rows.astype(jnp.float32)
    inverse_root_mean_square = lax.rsqrt(lax.optimization_barrier(jnp.mean(features * features, axis=1)) + EPSILON)
    normed = (features * inverse_root_mean_square[:, None] * norm_gain[None, :]).astype(jnp.bfloat16)
    width_part = normed.shape[1] // N_TP
    normalized_pieces = lax.optimization_barrier(normed).astype(jnp.float32).reshape(normed.shape[0], N_TP, width_part)
    weight_pieces = kv_weight.astype(jnp.float32).reshape(N_TP, width_part, kv_weight.shape[1])
    partial_products = jnp.einsum('mlj,lja->lma', normalized_pieces, weight_pieces).astype(jnp.bfloat16)
    projected = lax.optimization_barrier(jnp.sum(lax.optimization_barrier(partial_products).astype(jnp.float32), axis=0))
    projected = projected.reshape(normed.shape[0], KVH, 2, HD)
    rotated = rotate_keys(projected[:, :, 0], positions)
    return jnp.stack([rotated, projected[:, :, 1]], axis=2).astype(jnp.bfloat16)

def attend_rows(query_rows, kv_rows, visible):
    score_scale = query_rows.shape[-1] ** (-0.5)
    key_part = kv_rows[:, :, 0].astype(jnp.float32)
    value_part = kv_rows[:, :, 1].astype(jnp.float32)
    scores = jnp.einsum('rhgd,shd->rhgs', query_rows.astype(jnp.float32), key_part) * score_scale
    scores = jnp.where(visible[:, None, None, :], scores, NEG_FILL)
    top_score = lax.optimization_barrier(jnp.max(scores, axis=-1, keepdims=True))
    weights = jnp.exp(scores - top_score)
    weight_sum = lax.optimization_barrier(jnp.sum(weights, axis=-1))
    rounded = lax.optimization_barrier(weights.astype(jnp.bfloat16)).astype(jnp.float32)
    mixed_rows = jnp.einsum('rhgs,shd->rhgd', rounded, value_part)
    return (mixed_rows / weight_sum[..., None]).astype(jnp.bfloat16).reshape(query_rows.shape[0], -1)

def reference(hidden, norm_gain, kv_weight, queries, kv_cache, cache_len, block_table):
    group_size = QH // KVH
    row_ids = jnp.arange(ROWS, dtype=jnp.int32)
    hidden_view = hidden.reshape(2, N_PIPE, ROWS, D)
    query_view = queries.reshape(2, N_PIPE, ROWS, KVH, group_size, HD)
    cache_view = kv_cache.reshape(2, N_PIPE, CAP, KVH, 2, HD)
    length_view = cache_len.reshape(2, N_PIPE, ROWS)
    new_kv = []
    for pool_index in range(2):
        positions = length_view[pool_index] + (row_ids[None, :] if pool_index == 0 else 0)
        new_kv.append(lax.map(lambda packed: project_block(packed[0], norm_gain, kv_weight, packed[1]), (hidden_view[pool_index], positions.astype(jnp.int32))))
    block_ids = jnp.arange(NBLK, dtype=jnp.int32)
    prefix = length_view[0][:, 0]
    live_rows = jnp.where(block_ids[None, :] < CAP // BLK, jnp.clip(prefix[:, None] - block_ids[None, :] * BLK, 0, BLK), BLK).astype(jnp.int32)
    row_live = jnp.arange(BLK, dtype=jnp.int32)[None, None, :] < live_rows[:, :, None]
    shipment = jnp.concatenate([cache_view[0], new_kv[0]], axis=1).reshape(N_PIPE, NBLK, BLK, KVH * 2 * HD)
    shipment = jnp.where(row_live[..., None], shipment, jnp.zeros_like(shipment)).reshape(N_PIPE, NBLK, BLK * KVH * 2 * HD)
    owners = block_table.reshape(N_PIPE, NBLK).astype(jnp.int32)
    onehot = (owners[:, :, None] == jnp.arange(N_PIPE, dtype=jnp.int32)[None, None, :]).astype(jnp.int32)
    cache_slot_index = lax.optimization_barrier(jnp.sum((jnp.cumsum(onehot, axis=1) - onehot) * onehot, axis=2)).astype(jnp.int32)
    sources = jnp.broadcast_to(jnp.arange(N_PIPE, dtype=jnp.int32)[:, None], (N_PIPE, NBLK))
    empty = jnp.zeros((N_PIPE, N_PIPE, CAPB, BLK * KVH * 2 * HD), jnp.bfloat16)
    incoming = empty.at[owners, sources, cache_slot_index].set(shipment)
    outgoing = empty.at[sources, owners, cache_slot_index].set(shipment)
    received = jnp.stack([outgoing, incoming]).reshape(2, N_PIPE * N_PIPE * CAPB * BLK, KVH * 2 * HD)

    def prefill_one(packed):
        query_rows, cache_rows, fresh_rows, lengths = packed
        kv_rows = jnp.concatenate([cache_rows, fresh_rows], axis=0)
        cache_visible = jnp.arange(CAP, dtype=jnp.int32)[None, :] < lengths[:, None]
        visible = jnp.concatenate([cache_visible, row_ids[None, :] <= row_ids[:, None]], axis=1)
        return attend_rows(query_rows, kv_rows, visible)

    def decode_one(packed):
        query_rows, cache_rows, fresh_rows, lengths = packed
        kv_rows = jnp.concatenate([cache_rows, fresh_rows], axis=0)
        cache_visible = jnp.arange(CAP, dtype=jnp.int32)[None, :] < lengths[:, None]
        visible = jnp.concatenate([cache_visible, row_ids[None, :] == row_ids[:, None]], axis=1)
        return attend_rows(query_rows, kv_rows, visible)
    prefill_out = lax.map(prefill_one, (query_view[0], cache_view[0], new_kv[0], length_view[0]))
    decode_out = lax.map(decode_one, (query_view[1], cache_view[1], new_kv[1], length_view[1]))
    attention = jnp.stack([prefill_out, decode_out]).reshape(2, N_PIPE * ROWS, QH * HD)
    return (attention, received)
```

```python
import jax
import jax.numpy as jnp
from jax import lax
from jax.experimental import pallas as pl
from jax.experimental.pallas import tpu as pltpu
from jax.sharding import PartitionSpec as P

D = 8192
QH = 64
KVH = 8
HD = 128
ROWS = 256
CAP = 4096
BLK = 16
NBLK = 272
CAPB = 34
N_PIPE = 16
CBLK = CAP // BLK
SLOTS = N_PIPE * CAPB
DIGITS = 16
GROUP = QH // KVH

ROPE_BASE = 500000.0
EPSILON = 1e-05
NEG_FILL = -1e30
EXP_SCALE = HD**-0.5 * 1.4426950408889634
MIB = 1024 * 1024

VM = pl.BlockSpec(memory_space=pltpu.VMEM)
SM = pl.BlockSpec(memory_space=pltpu.SMEM)
ANY = pl.BlockSpec(memory_space=pl.ANY)


def params(mib=40):
    return pltpu.CompilerParams(vmem_limit_bytes=mib * MIB)


def cross(x):
    pairs = [(p, N_PIPE + (p ^ 8)) for p in range(N_PIPE)]
    return lax.ppermute(x, ("role", "pipe"), pairs)


def pipe_move(x, move):
    pairs = []
    for y in range(2):
        for c in range(4):
            for core in range(2):
                ny, nc, ncore = move(y, c, core)
                pairs.append(((y * 4 + c) * 2 + core, (ny * 4 + nc) * 2 + ncore))
    return lax.ppermute(x, "pipe", pairs)


def pipe_exchange(x):
    parts = x.reshape((N_PIPE, CAPB) + x.shape[1:])
    return lax.all_to_all(parts, "pipe", 0, 0, tiled=True).reshape(x.shape)


def project_kernel(h_ref, gain_ref, w_ref, out_ref, scaled, digits):
    @pl.when(pl.program_id(0) == 0)
    def _():
        h = h_ref[...].astype(jnp.float32)
        scaled[...] = (h * gain_ref[...]).astype(jnp.bfloat16)
        total = jnp.sum(h * h, axis=1, keepdims=True)
        across = jnp.transpose(jnp.broadcast_to(total, (ROWS, 128)))
        rest = across[0:1, :] * (2.0**-27)
        rows = []
        for _ in range(DIGITS):
            rest = rest * 32.0
            digit = jnp.floor(rest)
            rest = rest - digit
            rows.append(digit)
        digits[...] = jnp.concatenate(rows, axis=0).astype(jnp.bfloat16)

    out_ref[0, :ROWS, :] = jnp.dot(
        scaled[...], w_ref[...], preferred_element_type=jnp.float32
    ).astype(jnp.bfloat16)
    out_ref[0, ROWS:, :] = digits[...]


def project(hidden, gain, weight):
    feats = hidden.shape[1]
    heads = weight.shape[1] // (2 * HD)
    return pl.pallas_call(
        project_kernel,
        grid=(heads,),
        in_specs=[
            pl.BlockSpec((ROWS, feats), lambda i: (0, 0)),
            pl.BlockSpec((1, feats), lambda i: (0, 0)),
            pl.BlockSpec((feats, 2 * HD), lambda i: (0, i)),
        ],
        out_specs=pl.BlockSpec((1, ROWS + DIGITS, 2 * HD), lambda i: (i, 0, 0)),
        out_shape=jax.ShapeDtypeStruct((heads, ROWS + DIGITS, 2 * HD), jnp.bfloat16),
        scratch_shapes=[
            pltpu.VMEM((ROWS, feats), jnp.bfloat16),
            pltpu.VMEM((DIGITS, ROWS), jnp.bfloat16),
        ],
        compiler_params=params(),
        name="project",
    )(hidden, gain, weight)


def fresh_kernel(sum_ref, cos_ref, sin_ref, out_ref):
    digits = sum_ref[ROWS:, :].astype(jnp.float32)
    total = jnp.zeros((1, ROWS), jnp.float32)
    for k in range(DIGITS - 1, -1, -1):
        total = total + digits[k : k + 1, :] * (2.0 ** (27 - 5 * (k + 1)))
    inverse = lax.rsqrt(total / D + EPSILON)
    inverse = jnp.transpose(jnp.broadcast_to(inverse, (HD, ROWS)))
    key = sum_ref[:ROWS, :HD].astype(jnp.float32) * inverse
    value = sum_ref[:ROWS, HD:].astype(jnp.float32) * inverse
    key = key * cos_ref[...] + pltpu.roll(key, HD // 2, 1) * sin_ref[...]
    out_ref[:, :HD] = key.astype(jnp.bfloat16)
    out_ref[:, HD:] = value.astype(jnp.bfloat16)


def fresh_rows(summed, cosine, sine):
    return pl.pallas_call(
        fresh_kernel,
        in_specs=[VM, VM, VM],
        out_specs=VM,
        out_shape=jax.ShapeDtypeStruct((ROWS, 2 * HD), jnp.bfloat16),
        compiler_params=params(),
        name="fresh",
    )(summed, cosine, sine)


def index_kernel(info_ref, table_ref, out_ref):
    role = info_ref[0]
    me = info_ref[1]
    other = lax.rem(me + 8, N_PIPE)
    table = table_ref[...]
    block = lax.broadcasted_iota(jnp.int32, (NBLK, 1), 0)
    earlier = (
        lax.broadcasted_iota(jnp.int32, (NBLK, NBLK), 1)
        < lax.broadcasted_iota(jnp.int32, (NBLK, NBLK), 0)
    ).astype(jnp.bfloat16)
    owner_ids = lax.broadcasted_iota(jnp.int32, (NBLK, N_PIPE), 1)
    slot_ids = lax.broadcasted_iota(jnp.int32, (1, SLOTS), 1)
    sent_row = jnp.where(role == 0, me, other)
    turn = jnp.where(role == 0, 8, 0)
    sent = jnp.zeros((NBLK, 1), jnp.int32)
    own = jnp.zeros((NBLK, 1), jnp.int32)
    fresh = jnp.full((BLK, SLOTS), -1, jnp.int32)
    fresh_block = lax.broadcasted_iota(jnp.int32, (BLK, 1), 0)
    for p in range(N_PIPE):
        column = table[:, p : p + 1]
        onehot = column == owner_ids
        before = jnp.dot(
            earlier, onehot.astype(jnp.bfloat16), preferred_element_type=jnp.float32
        )
        slot = jnp.sum(jnp.where(onehot, before, 0.0), axis=1, keepdims=True)
        slot = slot.astype(jnp.int32)
        target = lax.rem(column + turn, N_PIPE) * CAPB + slot
        sent = jnp.where(sent_row == p, target, sent)
        own = jnp.where(me == p, column * CAPB + slot, own)
        place = jnp.where(column == me, p * CAPB + slot, -1)[CBLK:, :]
        fresh = jnp.where(place == slot_ids, fresh_block + p * BLK, fresh)

    def source(target):
        return jnp.max(jnp.where(target == slot_ids, block, -1), axis=0, keepdims=True)

    sent_source = source(sent)
    out_ref[0:1, :] = jnp.where(
        jnp.logical_and(sent_source >= 0, sent_source < CBLK), sent_source, CBLK
    )
    own_source = source(own)
    own_cached = jnp.where(
        jnp.logical_and(own_source >= 0, own_source < CBLK), own_source, SLOTS
    )
    turned = lax.rem(slot_ids + 8 * CAPB, SLOTS)
    out_ref[1:2, :] = jnp.where(role == 0, own_cached, turned)
    out_ref[2:3, :] = jnp.where(role == 0, own_cached, slot_ids)
    out_ref[3:4, :] = jnp.where(
        role == 0,
        jnp.maximum(own_source - CBLK, -1),
        jnp.max(fresh, axis=0, keepdims=True),
    )


def slot_index(info, table):
    return pl.pallas_call(
        index_kernel,
        in_specs=[SM, VM],
        out_specs=VM,
        out_shape=jax.ShapeDtypeStruct((4, SLOTS), jnp.int32),
        compiler_params=params(),
        name="slot_index",
    )(info, table)


def dispatch_kernel(info_ref, index_ref, own_ref, crossed_ref, out_ref, held, sem):
    @pl.when(info_ref[0] == 0)
    def _():
        copy = pltpu.make_async_copy(own_ref, held.at[pl.ds(0, CBLK)], sem)
        copy.start()
        copy.wait()

    @pl.when(info_ref[0] != 0)
    def _():
        copy = pltpu.make_async_copy(crossed_ref, held.at[pl.ds(0, CBLK)], sem)
        copy.start()
        copy.wait()

    held[CBLK] = jnp.zeros(held.shape[1:], held.dtype)

    def step(r, _):
        out_ref[r] = held[index_ref[0, r]]
        return 0

    lax.fori_loop(0, SLOTS, step, 0, unroll=16)


def dispatch(info, index, own, crossed, name):
    shape = own.shape[1:]
    return pl.pallas_call(
        dispatch_kernel,
        in_specs=[SM, SM, ANY, ANY],
        out_specs=VM,
        out_shape=jax.ShapeDtypeStruct((SLOTS,) + shape, jnp.bfloat16),
        scratch_shapes=[
            pltpu.VMEM((CBLK + 1,) + shape, jnp.bfloat16),
            pltpu.SemaphoreType.DMA,
        ],
        compiler_params=params(),
        name=name,
    )(info, index, own, crossed)


def place_kernel(info_ref, index_ref, *refs):
    own = refs[0:3]
    got = refs[3:6]
    own_fresh = refs[6]
    pieces = refs[7:15]
    partner_ref = refs[15]
    out_ref = refs[16]
    held = refs[17:20]
    fresh = refs[20]
    sems = refs[21]
    me = info_ref[1]
    y = lax.div(me, 8)
    column = lax.rem(lax.div(me, 2), 4)
    core = lax.rem(me, 2)

    @pl.when(info_ref[0] == 0)
    def _():
        copies = [
            pltpu.make_async_copy(own[k], held[k].at[pl.ds(0, CBLK)], sems.at[k])
            for k in range(3)
        ]
        copies.append(pltpu.make_async_copy(own_fresh, fresh.at[pl.ds(0, BLK)], sems.at[3]))
        for copy in copies:
            copy.start()
        for copy in copies:
            copy.wait()

    @pl.when(info_ref[0] != 0)
    def _():
        copies = [
            pltpu.make_async_copy(got[k], held[k].at[pl.ds(0, SLOTS)], sems.at[k])
            for k in range(3)
        ]
        count = 3
        for k in range(16):
            row = k % 8
            owner_y = 1 - y if row < 4 else y
            owner_column = lax.rem(column + 4 - (0, 1, 3, 2)[row % 4], 4)
            owner_core = core if k < 8 else 1 - core
            owner = (owner_y * 4 + owner_column) * 2 + owner_core
            source = pieces[row] if k < 8 else partner_ref.at[row]
            copies.append(
                pltpu.make_async_copy(
                    source, fresh.at[pl.ds(owner * BLK, BLK)], sems.at[count]
                )
            )
            count += 1
        for copy in copies:
            copy.start()
        for copy in copies:
            copy.wait()

    for ref in held:
        ref[SLOTS] = jnp.zeros(ref.shape[1:], ref.dtype)

    def step(r, _):
        first = index_ref[1, r]
        new = index_ref[3, r]
        key = jnp.concatenate([held[0][first], held[1][index_ref[2, r]]], axis=0)
        old = jnp.concatenate([key, held[2][first]], axis=1)
        out_ref[r] = jnp.where(new >= 0, fresh[jnp.maximum(new, 0)], old)
        return 0

    lax.fori_loop(0, SLOTS, step, 0, unroll=8)


def place(info, index, own, got, own_fresh, pieces, partner):
    return pl.pallas_call(
        place_kernel,
        in_specs=[SM, SM] + [ANY] * 16,
        out_specs=VM,
        out_shape=jax.ShapeDtypeStruct((SLOTS, BLK, 2 * HD), jnp.bfloat16),
        scratch_shapes=[
            pltpu.VMEM((SLOTS + 1, BLK // 2, HD), jnp.bfloat16),
            pltpu.VMEM((SLOTS + 1, BLK // 2, HD), jnp.bfloat16),
            pltpu.VMEM((SLOTS + 1, BLK, HD), jnp.bfloat16),
            pltpu.VMEM((N_PIPE * BLK, BLK, 2 * HD), jnp.bfloat16),
            pltpu.SemaphoreType.DMA((20,)),
        ],
        compiler_params=params(),
        name="place",
    )(info, index, *own, *got, own_fresh, *pieces, partner)


KEYS = 512


def cached_kernel(q_ref, kv_ref, len_ref, sum_ref, top_ref, bias, values, scores):
    @pl.when(pl.program_id(0) == 0)
    def _():
        values[:, :HD] = kv_ref[:, HD:]
        values[:, HD:] = jnp.ones((CAP, HD), jnp.bfloat16)
        lengths = len_ref[...]
        for k in range(0, CAP, KEYS):
            ids = lax.broadcasted_iota(jnp.int32, (ROWS, KEYS), 1) + k
            bias[:, k : k + KEYS] = jnp.where(ids < lengths, 0.0, NEG_FILL)

    query = q_ref[...]
    top = jnp.full((ROWS, HD), NEG_FILL, jnp.float32)
    for k in range(0, CAP, KEYS):
        part = lax.dot_general(
            query,
            kv_ref[k : k + KEYS, :HD],
            (((1,), (1,)), ((), ())),
            preferred_element_type=jnp.float32,
        )
        part = part + bias[:, k : k + KEYS]
        scores[:, k : k + KEYS] = part
        for j in range(0, KEYS, HD):
            top = jnp.maximum(top, part[:, j : j + HD])
    top = jnp.max(top, axis=1, keepdims=True)
    total = jnp.zeros((ROWS, 2 * HD), jnp.float32)
    for k in range(0, CAP, KEYS):
        weights = jnp.exp2((scores[:, k : k + KEYS] - top) * EXP_SCALE)
        total = total + jnp.dot(
            weights.astype(jnp.bfloat16),
            values[k : k + KEYS, :],
            preferred_element_type=jnp.float32,
        )
    sum_ref[...] = total
    top_ref[...] = jnp.broadcast_to(top, (ROWS, HD))


def attend_cached(queries, cache, lengths, start, heads):
    return pl.pallas_call(
        cached_kernel,
        grid=(heads,),
        in_specs=[
            pl.BlockSpec((ROWS, HD), lambda i: (0, i + start)),
            pl.BlockSpec((CAP, 2 * HD), lambda i: (0, 0)),
            pl.BlockSpec((ROWS, 1), lambda i: (0, 0)),
        ],
        out_specs=[
            pl.BlockSpec((ROWS, 2 * HD), lambda i: (0, i)),
            pl.BlockSpec((ROWS, HD), lambda i: (0, i)),
        ],
        out_shape=[
            jax.ShapeDtypeStruct((ROWS, heads * 2 * HD), jnp.float32),
            jax.ShapeDtypeStruct((ROWS, heads * HD), jnp.float32),
        ],
        scratch_shapes=[
            pltpu.VMEM((ROWS, CAP), jnp.float32),
            pltpu.VMEM((CAP, 2 * HD), jnp.bfloat16),
            pltpu.VMEM((ROWS, CAP), jnp.float32),
        ],
        compiler_params=params(),
        name="attend_cached",
    )(queries, cache, lengths)


def join_kernel(info_ref, q_ref, fresh_ref, *refs):
    half = GROUP // 2
    sums, tops, out_ref = refs[0:2], refs[2:4], refs[4]
    row = lax.broadcasted_iota(jnp.int32, (ROWS, ROWS), 0)
    column = lax.broadcasted_iota(jnp.int32, (ROWS, ROWS), 1)
    bias = jnp.where(
        jnp.logical_and(column <= row, jnp.logical_or(info_ref[0] == 0, column == row)),
        0.0,
        NEG_FILL,
    )
    keys = fresh_ref[:, :HD]
    values = jnp.concatenate([fresh_ref[:, HD:], jnp.ones((ROWS, HD), jnp.bfloat16)], axis=1)
    for head in range(GROUP):
        j = head % half
        scores = lax.dot_general(
            q_ref[:, head * HD : (head + 1) * HD],
            keys,
            (((1,), (1,)), ((), ())),
            preferred_element_type=jnp.float32,
        )
        scores = scores + bias
        old_top = tops[head // half][:, j * HD : (j + 1) * HD]
        top = jnp.maximum(old_top, jnp.max(scores, axis=1, keepdims=True))
        keep = jnp.exp2((old_top - top) * EXP_SCALE)
        weights = jnp.exp2((scores - top[:, 0:1]) * EXP_SCALE).astype(jnp.bfloat16)
        new = jnp.dot(weights, values, preferred_element_type=jnp.float32)
        old = sums[head // half][:, 2 * j * HD : 2 * (j + 1) * HD]
        mixed = old[:, :HD] * keep + new[:, :HD]
        total = old[:, HD:] * keep + new[:, HD:]
        out_ref[:, head * HD : (head + 1) * HD] = (mixed / total).astype(jnp.bfloat16)


def join(info, queries, fresh, first, second):
    return pl.pallas_call(
        join_kernel,
        in_specs=[SM] + [VM] * 6,
        out_specs=VM,
        out_shape=jax.ShapeDtypeStruct((ROWS, GROUP * HD), jnp.bfloat16),
        compiler_params=params(),
        name="attend_join",
    )(info, queries, fresh, first[0], second[0], first[1], second[1])


def local(hidden, norm_gain, kv_weight, queries, kv_cache, cache_len, block_table):
    cache = kv_cache[0]
    query_rows = queries[0]
    lengths = cache_len[0]
    role = lax.axis_index("role")
    me = lax.axis_index("pipe")
    info = jnp.stack([role, me]).astype(jnp.int32)
    row_ids = jnp.arange(ROWS, dtype=jnp.int32)

    blocks = cache.reshape(CBLK, BLK, 2 * HD)
    live = (jnp.arange(CAP, dtype=jnp.int32) < lengths[0]).reshape(CBLK, BLK, 1)
    zero = jnp.zeros((), jnp.bfloat16)
    upper = jnp.where(live[:, :8], blocks[:, :8, :HD], zero)
    lower = jnp.where(live[:, 8:], blocks[:, 8:, :HD], zero)
    value = jnp.where(live, blocks[:, :, HD:], zero)
    upper_crossed = cross(upper)
    value_crossed = cross(value)

    tables = lax.all_to_all(
        jnp.broadcast_to(block_table[None], (N_PIPE, NBLK)), "pipe", 0, 0, tiled=True
    )
    index = slot_index(info, tables.T)

    payload = project(hidden[0], norm_gain[None], kv_weight)
    summed = lax.psum_scatter(
        payload.reshape(-1, 2 * HD), "tp", scatter_dimension=0, tiled=True
    )
    positions = lengths + jnp.where(role == 0, row_ids, 0)
    frequency = ROPE_BASE ** (-2.0 * jnp.arange(HD // 2, dtype=jnp.float32) / HD)
    angles = positions.astype(jnp.float32)[:, None] * frequency[None, :]
    cosine = jnp.cos(angles)
    sine = jnp.sin(angles)
    cosine = jnp.concatenate([cosine, cosine], axis=1)
    sine = jnp.concatenate([-sine, sine], axis=1)

    half = GROUP // 2
    column = lengths[:, None]
    first = attend_cached(query_rows, cache, column, 0, half)

    sent_upper = dispatch(info, index, lower, upper_crossed, "dispatch_upper")
    got_upper = pipe_exchange(sent_upper)
    got_lower = cross(got_upper)

    second = attend_cached(query_rows, cache, column, half, half)

    sent_value = dispatch(info, index, value, value_crossed, "dispatch_value")
    got_value = pipe_exchange(sent_value)

    fresh = fresh_rows(summed, cosine, sine)
    fresh_blocks = fresh.reshape(BLK, BLK, 2 * HD)
    moved = cross(fresh_blocks)
    near = [moved] + [
        pipe_move(moved, lambda y, c, core, d=d: (y, (c + d) % 4, core)) for d in (1, 3, 2)
    ]
    far = [pipe_move(x, lambda y, c, core: (1 - y, c, core)) for x in near]
    pieces = near + far
    partner = pipe_move(jnp.stack(pieces), lambda y, c, core: (y, c, 1 - core))

    attention = join(info, query_rows, fresh, first, second)
    received = place(
        info,
        index,
        (upper, lower, value),
        (got_upper, got_lower, got_value),
        fresh_blocks,
        pieces,
        partner,
    )
    return (attention[None], received.reshape(1, SLOTS * BLK, 2 * HD))


def solution(mesh):
    in_specs = (
        P("role", "pipe", "tp"),
        P("tp"),
        P("tp", None),
        P("role", "pipe", "tp"),
        P("role", "pipe", "tp"),
        P("role", "pipe"),
        P("pipe"),
    )
    out_specs = (P("role", "pipe", "tp"), P("role", "pipe", "tp"))
    return jax.shard_map(local, mesh=mesh, in_specs=in_specs, out_specs=out_specs, check_vma=False)
```

```python
import functools

import jax
import jax.numpy as jnp
from jax import lax
from jax.experimental import pallas as pl
from jax.experimental.pallas import tpu as pltpu
from jax.sharding import PartitionSpec as P

D = 8192
QH = 64
KVH = 8
HD = 128
ROWS = 256
CAP = 4096
BLK = 16
NBLK = 272
CAPB = 34
N_PIPE = 16
CBLK = CAP // BLK
SLOTS = N_PIPE * CAPB
DIGITS = 16
GROUP = QH // KVH

ROPE_BASE = 500000.0
EPSILON = 1e-05
NEG_FILL = -1e30
EXP_SCALE = HD**-0.5 * 1.4426950408889634
MIB = 1024 * 1024

VM = pl.BlockSpec(memory_space=pltpu.VMEM)
SM = pl.BlockSpec(memory_space=pltpu.SMEM)
HB = pl.BlockSpec(memory_space=pltpu.HBM)


class Chain:
    def __init__(self):
        self.token = None

    def __call__(self, kernel, operands, specs, out_specs, out_shape, scratch=(), name=None, mib=16, aliases=None):
        count = len(operands)
        outs = len(out_shape)
        extra = 0 if self.token is None else 1
        token = jax.ShapeDtypeStruct((8, 128), jnp.float32)

        def body(*refs):
            given, rest = refs[:count], refs[count + extra :]
            rest[outs][...] = jnp.zeros((8, 128), jnp.float32)
            kernel(*given, *rest[:outs], *rest[outs + 1 :])

        tokens = () if self.token is None else (self.token,)
        results = pl.pallas_call(
            body,
            in_specs=list(specs) + [VM] * extra,
            out_specs=list(out_specs) + [VM],
            out_shape=list(out_shape) + [token],
            scratch_shapes=list(scratch),
            compiler_params=pltpu.CompilerParams(vmem_limit_bytes=mib * MIB),
            cost_estimate=pl.CostEstimate(flops=1, bytes_accessed=1, transcendentals=0),
            input_output_aliases=aliases or {},
            name=name,
        )(*operands, *tokens)
        self.token = results[-1]
        return results[:-1]


def like(shape, dtype=jnp.bfloat16):
    return jax.ShapeDtypeStruct(shape, dtype)


def run_copies(copies):
    for copy in copies:
        copy.start()
    for copy in copies:
        copy.wait()


def fenced(work, operands):
    shapes = jax.eval_shape(work, operands)

    def idle(_):
        return jax.tree.map(lambda x: jnp.zeros(x.shape, x.dtype), shapes)

    return lax.cond(lax.axis_index("role") < 2, work, idle, operands)


def cross(x, turn=8):
    pairs = [(p, N_PIPE + (p ^ turn)) for p in range(N_PIPE)]
    return lax.ppermute(x, ("role", "pipe"), pairs)


def pipe_move(x, move):
    pairs = []
    for y in range(2):
        for c in range(4):
            for core in range(2):
                target = move(y, c, core)
                if target is not None:
                    ny, nc, ncore = target
                    pairs.append(((y * 4 + c) * 2 + core, (ny * 4 + nc) * 2 + ncore))
    return lax.ppermute(x, "pipe", pairs)


def spread(x, k):
    def move(y, c, core):
        if core == 1:
            return 1 - y, (c + k) % 4, 1
        return (y, (c + k + 1) % 4, 0) if k < 3 else None

    return pipe_move(x, move)


def pipe_exchange(x):
    parts = x.reshape((N_PIPE, x.shape[0] // N_PIPE) + x.shape[1:])
    return lax.all_to_all(parts, "pipe", 0, 0, tiled=True).reshape(x.shape)


DISTANCES = (4, 3, 5, 2, 6, 1, 7, 0)


def project_kernel(h_ref, gain_ref, w_ref, *refs):
    high_ref, low_ref = refs[0:2]
    out_refs = refs[2:9]
    weight, sems = refs[9:]
    shard = lax.axis_index("tp")
    copies = []
    for k, distance in enumerate(DISTANCES):
        head = lax.rem(shard + distance, len(DISTANCES))
        columns = pl.ds(pl.multiple_of(head * 2 * HD, 2 * HD), 2 * HD)
        copies.append(
            pltpu.make_async_copy(w_ref.at[:, columns], weight.at[k], sems.at[k])
        )
        copies[-1].start()
    h = h_ref[...].astype(jnp.float32)
    scaled = (h * gain_ref[...]).astype(jnp.bfloat16)
    total = jnp.sum(h * h, axis=1, keepdims=True)
    across = jnp.transpose(jnp.broadcast_to(total, (ROWS, 128)))
    rest = across[0:1, :] * (2.0**-27)
    rows = []
    for _ in range(DIGITS):
        rest = rest * 32.0
        digit = jnp.floor(rest)
        rest = rest - digit
        rows.append(digit)
    digits = jnp.concatenate(rows, axis=0).astype(jnp.bfloat16)
    for k in range(len(DISTANCES)):
        copies[k].wait()
        piece = jnp.dot(scaled, weight[k], preferred_element_type=jnp.float32).astype(
            jnp.bfloat16
        )
        if k == 0:
            high_ref[...] = piece[:HD]
            low_ref[: ROWS - HD, :] = piece[HD:]
            low_ref[ROWS - HD :, :] = digits
        else:
            out_refs[k - 1][:ROWS, :] = piece
            out_refs[k - 1][ROWS:, :] = digits


def project(chain, hidden, gain, weight):
    feats = hidden.shape[1]
    count = len(DISTANCES)
    return chain(
        project_kernel,
        (hidden, gain, weight),
        [VM, VM, HB],
        [VM] * (count + 1),
        [like((HD, 2 * HD)), like((ROWS + DIGITS - HD, 2 * HD))]
        + [like((ROWS + DIGITS, 2 * HD))] * (count - 1),
        [
            pltpu.VMEM((count, feats, 2 * HD), jnp.bfloat16),
            pltpu.SemaphoreType.DMA((count,)),
        ],
        name="project",
        mib=60,
    )


def ring_shift(high, low):
    devices = lax.axis_size("tp")
    up = [(i, (i + 1) % devices) for i in range(devices)]
    down = [(i, (i - 1) % devices) for i in range(devices)]
    return lax.ppermute(high, "tp", up), lax.ppermute(low, "tp", down)


def add_kernel(high_ref, low_ref, one_ref, two_ref, high_out, low_out):
    rows = high_ref.shape[0]
    high_out[:rows, :] = one_ref[:rows, :] + high_ref[...]
    if rows < ROWS:
        high_out[rows:, :] = one_ref[rows:, :]
        low_out[:rows, :] = two_ref[:rows, :]
        low_out[rows:, :] = two_ref[rows:, :] + low_ref[...]
    else:
        low_out[...] = two_ref[...] + low_ref[...]


def add_step(chain, high, low, one, two):
    return chain(
        add_kernel,
        (high, low, one, two),
        [VM] * 4,
        [VM] * 2,
        [like((ROWS + DIGITS, 2 * HD))] * 2,
        name="add_step",
    )


def fresh_kernel(mine_ref, high_ref, low_ref, cos_ref, sin_ref, whole_out, upper_out, lower_out, value_out):
    summed = mine_ref[...].astype(jnp.float32) + high_ref[...].astype(jnp.float32)
    summed = summed + low_ref[...].astype(jnp.float32)
    digits = summed[ROWS:, :]
    total = jnp.zeros((1, ROWS), jnp.float32)
    for k in range(DIGITS - 1, -1, -1):
        total = total + digits[k : k + 1, :] * (2.0 ** (27 - 5 * (k + 1)))
    inverse = lax.rsqrt(total / D + EPSILON)
    inverse = jnp.transpose(jnp.broadcast_to(inverse, (HD, ROWS)))
    key = summed[:ROWS, :HD] * inverse
    value = summed[:ROWS, HD:] * inverse
    key = key * cos_ref[...] + pltpu.roll(key, HD // 2, 1) * sin_ref[...]
    key = key.astype(jnp.bfloat16).reshape(BLK, BLK, HD)
    value = value.astype(jnp.bfloat16).reshape(BLK, BLK, HD)
    whole_out[:, :, :HD] = key
    whole_out[:, :, HD:] = value
    upper_out[...] = key[:, : BLK // 2]
    lower_out[...] = key[:, BLK // 2 :]
    value_out[...] = value


def fresh_rows(chain, mine, high, low, cosine, sine):
    half = like((BLK, BLK // 2, HD))
    return chain(
        fresh_kernel,
        (mine, high, low, cosine, sine),
        [VM] * 5,
        [VM] * 4,
        [like((BLK, BLK, 2 * HD)), half, half, like((BLK, BLK, HD))],
        name="fresh",
    )


def pack(chain, parts, passed=(), stand_in=None):
    shape = (parts[0].shape[0] * len(parts),) + parts[0].shape[1:]
    rows = parts[0].shape[0]
    count = len(parts)
    given = (*parts,) if stand_in is None else (*parts, stand_in)

    def kernel(*refs):
        out_ref = refs[len(given) + len(passed)]
        for k in range(count):
            out_ref[k * rows : (k + 1) * rows] = refs[k][...]
        if stand_in is not None:

            @pl.when(lax.rem(lax.axis_index("pipe"), 2) == 0)
            def _():
                out_ref[(count - 1) * rows :] = refs[count][...]

    return chain(
        kernel,
        (*given, *passed),
        [VM] * len(given) + [HB] * len(passed),
        [VM] + [HB] * len(passed),
        [like(shape)] + [pltpu.HBM(x.shape, x.dtype) for x in passed],
        name="pack",
        aliases={len(given) + k: 1 + k for k in range(len(passed))},
    )


SEGMENTS = 4
NOTED = CAPB + 1


def live_kernel(outs, len_ref, cache_ref, *refs):
    targets, held, sources, sems = refs[: len(outs)], refs[-2 - len(outs)], refs[-1 - len(outs) : -1], refs[-1]
    size = CBLK // SEGMENTS
    loads = []
    first_column = min(column for _, _, column in outs)
    width = held.shape[2]
    for k in range(SEGMENTS):
        part = pl.ds(k * size, size)
        loads.append(
            pltpu.make_async_copy(
                cache_ref.at[part, :, pl.ds(first_column, width)], held.at[part], sems.at[0, k]
            )
        )
        loads[-1].start()
    block = lax.broadcasted_iota(jnp.int32, (size, BLK, HD), 0)
    row = lax.broadcasted_iota(jnp.int32, (size, BLK, HD), 1) + block * BLK
    zero = jnp.zeros((), jnp.bfloat16)
    stores = []
    for k in range(SEGMENTS):
        part = pl.ds(k * size, size)
        loads[k].wait()
        live = row < len_ref[0, 0] - k * size * BLK
        for j, (start, stop, column) in enumerate(outs):
            columns = slice(column - first_column, column - first_column + HD)
            rows = jnp.where(live, held[part, :, columns], zero)
            sources[j][part] = rows[:, start:stop]
            stores.append(
                pltpu.make_async_copy(
                    sources[j].at[part], targets[j].at[part], sems.at[j + 1, k]
                )
            )
            stores[-1].start()
    for store in stores:
        store.wait()


def upper_kernel(len_ref, cache_ref, table_ref, out_ref, table_out, held, source, noted, sems):
    table = table_ref[...].reshape(1, NBLK).astype(jnp.float32)
    rest = jnp.concatenate(
        [table[:, 2 * HD :], jnp.zeros((1, 3 * HD - NBLK), jnp.float32)], axis=1
    )
    rows = [table[:, :HD], table[:, HD : 2 * HD], rest, jnp.zeros((5, HD), jnp.float32)]
    noted[0] = jnp.concatenate(rows, axis=0).astype(jnp.bfloat16)
    table_out[...] = noted[0]
    note = pltpu.make_async_copy(noted, out_ref.at[pl.ds(CBLK, 1)], sems.at[2, 0])
    note.start()
    live_kernel(((0, BLK // 2, 0),), len_ref, cache_ref, out_ref, held, source, sems)
    note.wait()


def live_upper(chain, cache_len, blocks, table):
    half = (CBLK, BLK // 2, HD)
    return chain(
        upper_kernel,
        (cache_len, blocks, table),
        [SM, HB, VM],
        [HB, VM],
        [pltpu.HBM((CBLK + 1, BLK // 2, HD), jnp.bfloat16), like((BLK // 2, HD))],
        [
            pltpu.VMEM((CBLK, BLK, HD), jnp.bfloat16),
            pltpu.VMEM(half, jnp.bfloat16),
            pltpu.VMEM((1, BLK // 2, HD), jnp.bfloat16),
            pltpu.SemaphoreType.DMA((3, SEGMENTS)),
        ],
        name="live_upper",
        mib=60,
    )


def live_rest(chain, cache_len, blocks):
    outs = ((BLK // 2, BLK, 0), (0, BLK // 2, HD), (BLK // 2, BLK, HD), (0, BLK, HD))
    shapes = [(CBLK, stop - start, HD) for start, stop, _ in outs]
    return chain(
        functools.partial(live_kernel, outs),
        (cache_len, blocks),
        [SM, HB],
        [HB] * len(outs),
        [pltpu.HBM(shape, jnp.bfloat16) for shape in shapes],
        [pltpu.VMEM(blocks.shape, jnp.bfloat16)]
        + [pltpu.VMEM(shape, jnp.bfloat16) for shape in shapes]
        + [pltpu.SemaphoreType.DMA((1 + len(outs), SEGMENTS))],
        name="live_rest",
        mib=32,
    )


def write_index(own_ref, table_ref, out_ref, note_ref):
    role = lax.axis_index("role")

    def column_rows(block):
        row = jnp.concatenate([block[0:1], block[1:2], block[2:3, : NBLK - 2 * HD]], axis=1)
        return jnp.broadcast_to(row, (8, NBLK))

    own_block = own_ref[...].astype(jnp.float32)
    sent_block = jnp.where(role == 0, own_block, table_ref[0].astype(jnp.float32))
    rows = jnp.concatenate([column_rows(own_block), column_rows(sent_block)], axis=0)
    tables = jnp.transpose(rows)
    own = tables[:, 0:1]
    sent = tables[:, 8:9]
    ids = lax.broadcasted_iota(jnp.int32, (NBLK, N_PIPE), 1).astype(jnp.float32)
    earlier = (
        lax.broadcasted_iota(jnp.int32, (NBLK, NBLK), 1)
        < lax.broadcasted_iota(jnp.int32, (NBLK, NBLK), 0)
    ).astype(jnp.bfloat16)

    def slots(column):
        onehot = column == ids
        before = jnp.dot(
            earlier, onehot.astype(jnp.bfloat16), preferred_element_type=jnp.float32
        )
        return jnp.sum(jnp.where(onehot, before, 0.0), axis=1, keepdims=True)

    own_slot = slots(own)
    sent_slot = slots(sent)
    turned = jnp.where(role == 0, jnp.where(sent >= 8.0, sent - 8.0, sent + 8.0), sent)
    slot_ids = lax.broadcasted_iota(jnp.int32, (1, SLOTS), 1)
    block = lax.broadcasted_iota(jnp.int32, (NBLK, 1), 0)

    def source(owner, slot):
        target = (owner * float(CAPB) + slot).astype(jnp.int32)
        return jnp.max(jnp.where(target == slot_ids, block, -1), axis=0, keepdims=True)

    sent_source = source(turned, sent_slot)
    out_ref[0:1, :] = jnp.where(sent_source < 0, NBLK, sent_source)
    own_source = source(own, own_slot)
    group = lax.div(slot_ids, CAPB)
    noted = slot_ids + group
    turned_ids = lax.rem(slot_ids + 8 * CAPB, SLOTS)
    turned_noted = lax.rem(noted + 8 * NOTED, N_PIPE * NOTED)
    own_noted = jnp.where(own_source < 0, N_PIPE * NOTED, own_source)
    out_ref[1:2, :] = jnp.where(role == 0, own_noted, turned_noted)
    out_ref[2:3, :] = jnp.where(role == 0, own_noted, noted)
    out_ref[3:4, :] = jnp.where(
        role == 0, jnp.where(own_source < 0, SLOTS, own_source), turned_ids
    )

    lanes = lax.broadcasted_iota(jnp.int32, (BLK, HD), 1)
    both = jnp.where(lanes == 0, sent_slot[CBLK:, :], sent[CBLK:, :])
    both = jnp.concatenate([both, jnp.full((HD - BLK, HD), -1.0, jnp.float32)], axis=0)
    both = jnp.transpose(both)
    for q in range(N_PIPE):
        note = jnp.where(both[1:2, :] == float(q), both[0:1, :], -1.0)
        note_ref[q] = jnp.broadcast_to(note, (BLK // 2, HD)).astype(jnp.bfloat16)


def fill_slots(index_ref, held, filled, out_ref, sems, note_ref=None):
    stride = CAPB if note_ref is None else NOTED
    for ref in held:
        ref[pl.ds(CBLK, BLK + 1)] = jnp.zeros((BLK + 1,) + ref.shape[1:], ref.dtype)
    groups = N_PIPE // SEGMENTS
    copies = []
    for k in range(SEGMENTS):

        def group_step(g, _):
            for s in range(CAPB):
                i = index_ref[0, g * CAPB + s]
                for j, ref in enumerate(held):
                    filled[g * stride + s, j * BLK // 2 : (j + 1) * BLK // 2] = ref[i]
            if note_ref is not None:
                filled[g * stride + CAPB] = note_ref[g]
            return 0

        lax.fori_loop(k * groups, (k + 1) * groups, group_step, 0)
        part = pl.ds(k * groups * stride, groups * stride)
        copies.append(pltpu.make_async_copy(filled.at[part], out_ref.at[part], sems.at[k]))
        copies[-1].start()
    for copy in copies:
        copy.wait()


def first_kernel(
    own_table, own_ref, crossed_ref, out_ref, index_ref, held, table, note, filled, listed, sems
):
    role = lax.axis_index("role")
    cached = pl.ds(0, CBLK)
    tables = pltpu.make_async_copy(
        crossed_ref.at[pl.ds(CBLK, 1)], table, sems.at[SEGMENTS + 1]
    )
    tables.start()

    @pl.when(role == 0)
    def _():
        pltpu.make_async_copy(own_ref, held.at[cached], sems.at[SEGMENTS]).start()

    @pl.when(role != 0)
    def _():
        pltpu.make_async_copy(
            crossed_ref.at[cached], held.at[cached], sems.at[SEGMENTS]
        ).start()

    tables.wait()
    write_index(own_table, table, index_ref, note)
    listing = pltpu.make_async_copy(index_ref, listed, sems.at[SEGMENTS + 2])
    listing.start()
    pltpu.make_async_copy(own_ref, held.at[cached], sems.at[SEGMENTS]).wait()
    listing.wait()
    fill_slots(listed, (held,), filled, out_ref, sems, note)


def first_dispatch(chain, table, own, crossed):
    half = (BLK // 2, HD)
    entries = N_PIPE * NOTED
    return chain(
        first_kernel,
        (table, own, crossed),
        [VM, HB, HB],
        [HB, VM],
        [pltpu.HBM((entries,) + half, jnp.bfloat16), like((4, SLOTS), jnp.int32)],
        [
            pltpu.VMEM((NBLK + 1,) + half, jnp.bfloat16),
            pltpu.VMEM((1,) + half, jnp.bfloat16),
            pltpu.VMEM((N_PIPE,) + half, jnp.bfloat16),
            pltpu.VMEM((entries,) + half, jnp.bfloat16),
            pltpu.SMEM((4, SLOTS), jnp.int32),
            pltpu.SemaphoreType.DMA((SEGMENTS + 3,)),
        ],
        name="first_dispatch",
        mib=24,
    )


def second_kernel(index_ref, *refs):
    own, crossed, out_ref, held, filled, sems = refs[:2], refs[2:4], refs[4], refs[5:7], *refs[7:]
    cached = pl.ds(0, CBLK)

    def load(sources):
        run_copies(
            [
                pltpu.make_async_copy(sources[j], held[j].at[cached], sems.at[SEGMENTS + j])
                for j in range(2)
            ]
        )

    @pl.when(lax.axis_index("role") == 0)
    def _():
        load(own)

    @pl.when(lax.axis_index("role") != 0)
    def _():
        load(crossed)

    fill_slots(index_ref, held, filled, out_ref, sems)


def second_dispatch(chain, index, own, crossed):
    return chain(
        second_kernel,
        (index, *own, *crossed),
        [SM] + [HB] * 4,
        [HB],
        [pltpu.HBM((SLOTS, BLK, HD), jnp.bfloat16)],
        [pltpu.VMEM((NBLK + 1, BLK // 2, HD), jnp.bfloat16)] * 2
        + [
            pltpu.VMEM((SLOTS, BLK, HD), jnp.bfloat16),
            pltpu.SemaphoreType.DMA((SEGMENTS + 2,)),
        ],
        name="second_dispatch",
        mib=24,
    )[0]


def place_kernel(index_ref, *refs):
    own, own_fresh, got = refs[0:3], refs[3:6], refs[6:9]
    near_ref, far_ref, out_ref = refs[9:12]
    held = refs[12:15]
    filled, notes, places, sems, out_sems = refs[15:]
    role = lax.axis_index("role")
    me = lax.axis_index("pipe")
    y = lax.div(me, 8)
    column = lax.rem(lax.div(me, 2), 4)
    core = lax.rem(me, 2)
    groups = N_PIPE // SEGMENTS
    for ref in held:
        ref[ref.shape[0] - 1] = jnp.zeros(ref.shape[1:], ref.dtype)

    def loads(k):
        copies = []
        for j in range(3):
            stride = CAPB if j == 2 else NOTED
            turn = k if j == 1 else (k + 2) % SEGMENTS
            part = pl.ds(turn * groups * stride, groups * stride)
            copies.append(
                pltpu.make_async_copy(got[j].at[part], held[j].at[part], sems.at[j, k])
            )
        return copies

    def fill(k):
        def group_step(g, _):
            for s in range(CAPB):
                r = g * CAPB + s
                filled[r, : BLK // 2, :HD] = held[0][index_ref[1, r]]
                filled[r, BLK // 2 :, :HD] = held[1][index_ref[2, r]]
                filled[r, :, HD:] = held[2][index_ref[3, r]]
            return 0

        lax.fori_loop(k * groups, (k + 1) * groups, group_step, 0)

    def store(k):
        part = pl.ds(k * groups * CAPB, groups * CAPB)
        return pltpu.make_async_copy(filled.at[part], out_ref.at[part], out_sems.at[k])

    @pl.when(role == 0)
    def _():
        copies = []
        for j in range(3):
            copies.append(
                pltpu.make_async_copy(
                    own[j].at[pl.ds(0, CBLK)], held[j].at[pl.ds(0, CBLK)], sems.at[j, 0]
                )
            )
            copies.append(
                pltpu.make_async_copy(
                    own_fresh[j], held[j].at[pl.ds(CBLK, BLK)], sems.at[j, 1]
                )
            )
        run_copies(copies)
        for k in range(SEGMENTS):
            fill(k)
            store(k).start()
        for k in range(SEGMENTS):
            store(k).wait()

    @pl.when(role != 0)
    def _():
        arrivals = [loads(k) for k in range(SEGMENTS)]
        for j in range(3):
            for k in range(SEGMENTS):
                arrivals[k][j].start()
        for k in range(SEGMENTS):
            arrivals[k][0].wait()
        for i in range(N_PIPE):
            p = (i + 8) % N_PIPE
            slot = held[0][i * NOTED + CAPB][0:1, :].astype(jnp.float32)
            spot = jnp.where(slot >= 0.0, slot + float(p * CAPB), float(SLOTS))
            notes[p : p + 1, :] = spot.astype(jnp.int32)
        listing = pltpu.make_async_copy(notes, places, out_sems.at[SEGMENTS])
        listing.start()
        for k in range(SEGMENTS):
            arrivals[k][1].wait()
            arrivals[k][2].wait()
            fill(k)
        listing.wait()
        for side, ref in enumerate((near_ref, far_ref)):
            sender = core if side == 0 else 1 - core
            for k in range(4):
                for e in range(2):
                    owner_y = jnp.where(sender == 0, 1 - y, y)
                    back = jnp.where(sender == 0, k + 1, k)
                    owner_column = lax.rem(column + 4 - back, 4)
                    owner_core = sender if e == 0 else 1 - sender
                    owner = (owner_y * 4 + owner_column) * 2 + owner_core
                    row = (k * 2 + e) * BLK
                    for j in range(BLK):
                        filled[places[owner, j]] = ref[row + j]
        for k in range(SEGMENTS):
            store(k).start()
        for k in range(SEGMENTS):
            store(k).wait()


def place(chain, index, own, own_fresh, got, near, far):
    entries = N_PIPE * NOTED
    return chain(
        place_kernel,
        (index, *own, *own_fresh, *got, near, far),
        [SM] + [HB] * 3 + [VM] * 3 + [HB] * 3 + [VM] * 2,
        [HB],
        [pltpu.HBM((SLOTS, BLK, 2 * HD), jnp.bfloat16)],
        [
            pltpu.VMEM((entries + 1, BLK // 2, HD), jnp.bfloat16),
            pltpu.VMEM((entries + 1, BLK // 2, HD), jnp.bfloat16),
            pltpu.VMEM((SLOTS + 1, BLK, HD), jnp.bfloat16),
            pltpu.VMEM((SLOTS + 1, BLK, 2 * HD), jnp.bfloat16),
            pltpu.VMEM((N_PIPE, HD), jnp.int32),
            pltpu.SMEM((N_PIPE, HD), jnp.int32),
            pltpu.SemaphoreType.DMA((3, SEGMENTS)),
            pltpu.SemaphoreType.DMA((SEGMENTS + 1,)),
        ],
        name="place",
        mib=56,
    )[0]


TOTAL = CAP + ROWS
CHUNKS = tuple((k, 512) for k in range(0, CAP, 512)) + ((CAP, ROWS),)


def attend_kernel(start, heads, q_ref, kv_ref, fresh_ref, len_ref, *refs):
    out_ref, bias, keys, values, first, second, mixed, sem = refs[-8:]
    keys[:CAP, :] = kv_ref[:, :HD]
    keys[CAP:, :] = fresh_ref[:, :, :HD].reshape(ROWS, HD)
    values[:CAP, :HD] = kv_ref[:, HD:]
    values[CAP:, :HD] = fresh_ref[:, :, HD:].reshape(ROWS, HD)
    values[:, HD:] = jnp.ones((TOTAL, HD), jnp.bfloat16)
    lengths = jnp.transpose(jnp.broadcast_to(len_ref[...].astype(jnp.float32), (HD, ROWS)))
    ids = lax.broadcasted_iota(jnp.int32, (ROWS, HD), 1).astype(jnp.float32)
    for k in range(0, CAP, HD):
        bias[:, k : k + HD] = jnp.where(ids + float(k) < lengths, 0.0, NEG_FILL)
    row = lax.broadcasted_iota(jnp.int32, (ROWS, ROWS), 0)
    column = lax.broadcasted_iota(jnp.int32, (ROWS, ROWS), 1)
    prefill = lax.axis_index("role") == 0
    bias[:, CAP:] = jnp.where(
        jnp.logical_and(column <= row, jnp.logical_or(prefill, column == row)), 0.0, NEG_FILL
    )
    held = (first, second)

    def score(head, k, size, top):
        part = lax.dot_general(
            q_ref[:, (start + head) * HD : (start + head + 1) * HD],
            keys[k : k + size, :],
            (((1,), (1,)), ((), ())),
            preferred_element_type=jnp.float32,
        )
        part = part + bias[:, k : k + size]
        held[head % 2][:, k : k + size] = part
        for j in range(0, size, HD):
            top = jnp.maximum(top, part[:, j : j + HD])
        return top

    def mix(head, k, size, top, total):
        weights = jnp.exp2((held[head % 2][:, k : k + size] - top) * EXP_SCALE)
        return total + jnp.dot(
            weights.astype(jnp.bfloat16),
            values[k : k + size, :],
            preferred_element_type=jnp.float32,
        )

    best = None
    for head in range(heads + 1):
        top = jnp.full((ROWS, HD), NEG_FILL, jnp.float32)
        total = jnp.zeros((ROWS, 2 * HD), jnp.float32)
        for k, size in CHUNKS:
            if head < heads:
                top = score(head, k, size, top)
            if head > 0:
                total = mix(head - 1, k, size, best, total)
        if head > 0:
            mixed[:, (head - 1) * HD : head * HD] = (
                total[:, :HD] / total[:, HD:]
            ).astype(jnp.bfloat16)
        if head < heads:
            best = jnp.max(top, axis=1, keepdims=True)
    columns = pl.ds(start * HD, heads * HD)
    run_copies([pltpu.make_async_copy(mixed, out_ref.at[:, columns], sem)])


def attend(chain, queries, cache, fresh, cache_len, start, heads, others=()):
    return chain(
        functools.partial(attend_kernel, start, heads),
        (queries, cache, fresh, cache_len, *others),
        [VM] * 4 + [HB] * len(others),
        [HB],
        [pltpu.HBM((ROWS, GROUP * HD), jnp.bfloat16)],
        [
            pltpu.VMEM((ROWS, TOTAL), jnp.float32),
            pltpu.VMEM((TOTAL, HD), jnp.bfloat16),
            pltpu.VMEM((TOTAL, 2 * HD), jnp.bfloat16),
            pltpu.VMEM((ROWS, TOTAL), jnp.float32),
            pltpu.VMEM((ROWS, TOTAL), jnp.float32),
            pltpu.VMEM((ROWS, heads * HD), jnp.bfloat16),
            pltpu.SemaphoreType.DMA,
        ],
        name="attend",
        mib=40,
        aliases={4: 0} if others else None,
    )[0]


def rotation(lengths):
    row_ids = jnp.arange(ROWS, dtype=jnp.int32)
    positions = lengths + jnp.where(lax.axis_index("role") == 0, row_ids, 0)
    frequency = ROPE_BASE ** (-2.0 * jnp.arange(HD // 2, dtype=jnp.float32) / HD)
    angles = positions.astype(jnp.float32)[:, None] * frequency[None, :]
    cosine, sine = jnp.cos(angles), jnp.sin(angles)
    return jnp.concatenate([cosine, cosine], axis=1), jnp.concatenate([-sine, sine], axis=1)


def local(hidden, norm_gain, kv_weight, queries, kv_cache, cache_len, block_table):
    chain = Chain()
    cache = kv_cache[0]
    query_rows = queries[0]
    blocks = cache.reshape(CBLK, BLK, 2 * HD)
    cosine, sine = rotation(cache_len[0])

    upper, table = live_upper(chain, cache_len, blocks, block_table)
    upper_crossed = cross(upper)
    lower, value_upper, value_lower, value = live_rest(chain, cache_len, blocks)
    halves = value_upper, value_lower
    halves_crossed = cross(value_upper), cross(value_lower)
    high, low, *sums = project(chain, hidden[0], norm_gain[None], kv_weight)

    def early(operands):
        table, lower, crossed, high, low, sums, chain.token = operands
        sent, index = first_dispatch(chain, table, lower, crossed)
        got = pipe_exchange(sent)
        high, low = ring_shift(high, low)
        for k in range(2):
            high, low = ring_shift(*add_step(chain, high, low, sums[2 * k], sums[2 * k + 1]))
        return index, got, high, low, chain.token

    operands = (table, lower, upper_crossed, high, low, sums[:4], chain.token)
    index, got_upper, high, low, chain.token = fenced(early, operands)
    sent_value = second_dispatch(chain, index, halves, halves_crossed)
    got_value = pipe_exchange(sent_value)

    def late(operands):
        high, low, sums, cosine, sine, chain.token = operands
        high, low = ring_shift(*add_step(chain, high, low, sums[0], sums[1]))
        fresh, *own_fresh = fresh_rows(chain, sums[2], high, low, cosine, sine)
        moved, beside = cross(fresh), cross(fresh, 9)
        attention = attend(chain, query_rows, cache, fresh, cache_len, 0, 4)
        return attention, fresh, own_fresh, moved, beside, chain.token

    got_lower = cross(got_upper)
    operands = (high, low, sums[4:], cosine, sine, chain.token)
    attention, fresh, own_fresh, moved, beside, chain.token = fenced(late, operands)
    pair, got_lower = pack(chain, (moved, beside), (got_lower,))
    reached = [spread(pair, k) for k in range(4)]
    attention = attend(chain, query_rows, cache, fresh, cache_len, 4, 2, (attention,))
    (near,) = pack(chain, reached, (), pair)
    far = pipe_move(near, lambda y, c, core: (y, c, 1 - core))
    attention = attend(chain, query_rows, cache, fresh, cache_len, 6, 2, (attention,))
    received = place(
        chain,
        index,
        (upper, lower, value),
        own_fresh,
        (got_upper, got_lower, got_value),
        near,
        far,
    )
    return (attention[None], received.reshape(1, SLOTS * BLK, 2 * HD))


def solution(mesh):
    in_specs = (
        P("role", "pipe", "tp"),
        P("tp"),
        P("tp", None),
        P("role", "pipe", "tp"),
        P("role", "pipe", "tp"),
        P("role", "pipe"),
        P("pipe"),
    )
    out_specs = (P("role", "pipe", "tp"), P("role", "pipe", "tp"))
    return jax.shard_map(local, mesh=mesh, in_specs=in_specs, out_specs=out_specs, check_vma=False)
```

```python
import functools

import jax
import jax.numpy as jnp
from jax import lax
from jax.experimental import pallas as pl
from jax.experimental.pallas import tpu as pltpu
from jax.sharding import PartitionSpec as P

D = 8192
QH = 64
KVH = 8
HD = 128
ROWS = 256
CAP = 4096
BLK = 16
NBLK = 272
CAPB = 34
N_PIPE = 16
CBLK = CAP // BLK
SLOTS = N_PIPE * CAPB
DIGITS = 16
GROUP = QH // KVH

ROPE_BASE = 500000.0
EPSILON = 1e-05
NEG_FILL = -1e30
EXP_SCALE = HD**-0.5 * 1.4426950408889634
MIB = 1024 * 1024

VM = pl.BlockSpec(memory_space=pltpu.VMEM)
SM = pl.BlockSpec(memory_space=pltpu.SMEM)
HB = pl.BlockSpec(memory_space=pltpu.HBM)


class Chain:
    def __init__(self):
        self.token = None

    def __call__(self, kernel, operands, specs, out_specs, out_shape, scratch=(), name=None, mib=16, aliases=None):
        count = len(operands)
        outs = len(out_shape)
        extra = 0 if self.token is None else 1
        token = jax.ShapeDtypeStruct((8, 128), jnp.float32)

        def body(*refs):
            given, rest = refs[:count], refs[count + extra :]
            rest[outs][...] = jnp.zeros((8, 128), jnp.float32)
            kernel(*given, *rest[:outs], *rest[outs + 1 :])

        tokens = () if self.token is None else (self.token,)
        results = pl.pallas_call(
            body,
            in_specs=list(specs) + [VM] * extra,
            out_specs=list(out_specs) + [VM],
            out_shape=list(out_shape) + [token],
            scratch_shapes=list(scratch),
            compiler_params=pltpu.CompilerParams(vmem_limit_bytes=mib * MIB),
            cost_estimate=pl.CostEstimate(flops=1, bytes_accessed=1, transcendentals=0),
            input_output_aliases=aliases or {},
            name=name,
        )(*operands, *tokens)
        self.token = results[-1]
        return results[:-1]


def like(shape, dtype=jnp.bfloat16):
    return jax.ShapeDtypeStruct(shape, dtype)


def run_copies(copies):
    for copy in copies:
        copy.start()
    for copy in copies:
        copy.wait()


def fenced(work, operands):
    shapes = jax.eval_shape(work, operands)

    def idle(_):
        return jax.tree.map(lambda x: jnp.zeros(x.shape, x.dtype), shapes)

    return lax.cond(lax.axis_index("role") < 2, work, idle, operands)


def cross(x, turn=8):
    pairs = [(p, N_PIPE + (p ^ turn)) for p in range(N_PIPE)]
    return lax.ppermute(x, ("role", "pipe"), pairs)


def pipe_move(x, move):
    pairs = []
    for y in range(2):
        for c in range(4):
            for core in range(2):
                target = move(y, c, core)
                if target is not None:
                    ny, nc, ncore = target
                    pairs.append(((y * 4 + c) * 2 + core, (ny * 4 + nc) * 2 + ncore))
    return lax.ppermute(x, "pipe", pairs)


def spread(x, k):
    def move(y, c, core):
        if core == 1:
            return 1 - y, (c + k) % 4, 1
        return (y, (c + k + 1) % 4, 0) if k < 3 else None

    return pipe_move(x, move)


def pipe_exchange(x):
    parts = x.reshape((N_PIPE, x.shape[0] // N_PIPE) + x.shape[1:])
    return lax.all_to_all(parts, "pipe", 0, 0, tiled=True).reshape(x.shape)


DISTANCES = (4, 3, 5, 2, 6, 1, 7, 0)


def project_kernel(h_ref, gain_ref, w_ref, *refs):
    high_ref, low_ref = refs[0:2]
    out_refs = refs[2:9]
    weight, sems = refs[9:]
    shard = lax.axis_index("tp")
    copies = []
    for k, distance in enumerate(DISTANCES):
        head = lax.rem(shard + distance, len(DISTANCES))
        columns = pl.ds(pl.multiple_of(head * 2 * HD, 2 * HD), 2 * HD)
        copies.append(
            pltpu.make_async_copy(w_ref.at[:, columns], weight.at[k], sems.at[k])
        )
        copies[-1].start()
    h = h_ref[...].astype(jnp.float32)
    scaled = (h * gain_ref[...]).astype(jnp.bfloat16)
    total = jnp.sum(h * h, axis=1, keepdims=True)
    across = jnp.transpose(jnp.broadcast_to(total, (ROWS, 128)))
    rest = across[0:1, :] * (2.0**-27)
    rows = []
    for _ in range(DIGITS):
        rest = rest * 32.0
        digit = jnp.floor(rest)
        rest = rest - digit
        rows.append(digit)
    digits = jnp.concatenate(rows, axis=0).astype(jnp.bfloat16)
    for k in range(len(DISTANCES)):
        copies[k].wait()
        piece = jnp.dot(scaled, weight[k], preferred_element_type=jnp.float32).astype(
            jnp.bfloat16
        )
        if k == 0:
            high_ref[...] = piece[:HD]
            low_ref[: ROWS - HD, :] = piece[HD:]
            low_ref[ROWS - HD :, :] = digits
        else:
            out_refs[k - 1][:ROWS, :] = piece
            out_refs[k - 1][ROWS:, :] = digits


def project(chain, hidden, gain, weight):
    feats = hidden.shape[1]
    count = len(DISTANCES)
    return chain(
        project_kernel,
        (hidden, gain, weight),
        [VM, VM, HB],
        [VM] * (count + 1),
        [like((HD, 2 * HD)), like((ROWS + DIGITS - HD, 2 * HD))]
        + [like((ROWS + DIGITS, 2 * HD))] * (count - 1),
        [
            pltpu.VMEM((count, feats, 2 * HD), jnp.bfloat16),
            pltpu.SemaphoreType.DMA((count,)),
        ],
        name="project",
        mib=60,
    )


def ring_shift(high, low):
    devices = lax.axis_size("tp")
    up = [(i, (i + 1) % devices) for i in range(devices)]
    down = [(i, (i - 1) % devices) for i in range(devices)]
    return lax.ppermute(high, "tp", up), lax.ppermute(low, "tp", down)


def add_kernel(high_ref, low_ref, one_ref, two_ref, high_out, low_out):
    rows = high_ref.shape[0]
    high_out[:rows, :] = one_ref[:rows, :] + high_ref[...]
    if rows < ROWS:
        high_out[rows:, :] = one_ref[rows:, :]
        low_out[:rows, :] = two_ref[:rows, :]
        low_out[rows:, :] = two_ref[rows:, :] + low_ref[...]
    else:
        low_out[...] = two_ref[...] + low_ref[...]


def add_step(chain, high, low, one, two):
    return chain(
        add_kernel,
        (high, low, one, two),
        [VM] * 4,
        [VM] * 2,
        [like((ROWS + DIGITS, 2 * HD))] * 2,
        name="add_step",
    )


def fresh_kernel(mine_ref, high_ref, low_ref, cos_ref, sin_ref, whole_out, upper_out, lower_out, value_out):
    summed = mine_ref[...].astype(jnp.float32) + high_ref[...].astype(jnp.float32)
    summed = summed + low_ref[...].astype(jnp.float32)
    digits = summed[ROWS:, :]
    total = jnp.zeros((1, ROWS), jnp.float32)
    for k in range(DIGITS - 1, -1, -1):
        total = total + digits[k : k + 1, :] * (2.0 ** (27 - 5 * (k + 1)))
    inverse = lax.rsqrt(total / D + EPSILON)
    inverse = jnp.transpose(jnp.broadcast_to(inverse, (HD, ROWS)))
    key = summed[:ROWS, :HD] * inverse
    value = summed[:ROWS, HD:] * inverse
    key = key * cos_ref[...] + pltpu.roll(key, HD // 2, 1) * sin_ref[...]
    key = key.astype(jnp.bfloat16).reshape(BLK, BLK, HD)
    value = value.astype(jnp.bfloat16).reshape(BLK, BLK, HD)
    whole_out[:, :, :HD] = key
    whole_out[:, :, HD:] = value
    upper_out[...] = key[:, : BLK // 2]
    lower_out[...] = key[:, BLK // 2 :]
    value_out[...] = value


def fresh_rows(chain, mine, high, low, cosine, sine):
    half = like((BLK, BLK // 2, HD))
    return chain(
        fresh_kernel,
        (mine, high, low, cosine, sine),
        [VM] * 5,
        [VM] * 4,
        [like((BLK, BLK, 2 * HD)), half, half, like((BLK, BLK, HD))],
        name="fresh",
    )


def pack(chain, parts, passed=(), stand_in=None):
    shape = (parts[0].shape[0] * len(parts),) + parts[0].shape[1:]
    rows = parts[0].shape[0]
    count = len(parts)
    given = (*parts,) if stand_in is None else (*parts, stand_in)

    def kernel(*refs):
        out_ref = refs[len(given) + len(passed)]
        for k in range(count):
            out_ref[k * rows : (k + 1) * rows] = refs[k][...]
        if stand_in is not None:

            @pl.when(lax.rem(lax.axis_index("pipe"), 2) == 0)
            def _():
                out_ref[(count - 1) * rows :] = refs[count][...]

    return chain(
        kernel,
        (*given, *passed),
        [VM] * len(given) + [HB] * len(passed),
        [VM] + [HB] * len(passed),
        [like(shape)] + [pltpu.HBM(x.shape, x.dtype) for x in passed],
        name="pack",
        aliases={len(given) + k: 1 + k for k in range(len(passed))},
    )


SEGMENTS = 4
NOTED = CAPB + 1


def live_kernel(outs, len_ref, cache_ref, *refs):
    targets, held, sources, sems = refs[: len(outs)], refs[-2 - len(outs)], refs[-1 - len(outs) : -1], refs[-1]
    size = CBLK // SEGMENTS
    loads = []
    first_column = min(column for _, _, column in outs)
    width = held.shape[2]
    for k in range(SEGMENTS):
        part = pl.ds(k * size, size)
        loads.append(
            pltpu.make_async_copy(
                cache_ref.at[part, :, pl.ds(first_column, width)], held.at[part], sems.at[0, k]
            )
        )
        loads[-1].start()
    block = lax.broadcasted_iota(jnp.int32, (size, BLK, HD), 0)
    row = lax.broadcasted_iota(jnp.int32, (size, BLK, HD), 1) + block * BLK
    zero = jnp.zeros((), jnp.bfloat16)
    stores = []
    for k in range(SEGMENTS):
        part = pl.ds(k * size, size)
        loads[k].wait()
        live = row < len_ref[0, 0] - k * size * BLK
        for j, (start, stop, column) in enumerate(outs):
            columns = slice(column - first_column, column - first_column + HD)
            rows = jnp.where(live, held[part, :, columns], zero)
            sources[j][part] = rows[:, start:stop]
            stores.append(
                pltpu.make_async_copy(
                    sources[j].at[part], targets[j].at[part], sems.at[j + 1, k]
                )
            )
            stores[-1].start()
    for store in stores:
        store.wait()


def upper_kernel(len_ref, cache_ref, table_ref, out_ref, table_out, held, source, noted, sems):
    table = table_ref[...].reshape(1, NBLK).astype(jnp.float32)
    rest = jnp.concatenate(
        [table[:, 2 * HD :], jnp.zeros((1, 3 * HD - NBLK), jnp.float32)], axis=1
    )
    rows = [table[:, :HD], table[:, HD : 2 * HD], rest, jnp.zeros((5, HD), jnp.float32)]
    noted[0] = jnp.concatenate(rows, axis=0).astype(jnp.bfloat16)
    table_out[...] = noted[0]
    note = pltpu.make_async_copy(noted, out_ref.at[pl.ds(CBLK, 1)], sems.at[2, 0])
    note.start()
    live_kernel(((0, BLK // 2, 0),), len_ref, cache_ref, out_ref, held, source, sems)
    note.wait()


def live_upper(chain, cache_len, blocks, table):
    half = (CBLK, BLK // 2, HD)
    return chain(
        upper_kernel,
        (cache_len, blocks, table),
        [SM, HB, VM],
        [HB, VM],
        [pltpu.HBM((CBLK + 1, BLK // 2, HD), jnp.bfloat16), like((BLK // 2, HD))],
        [
            pltpu.VMEM((CBLK, BLK, HD), jnp.bfloat16),
            pltpu.VMEM(half, jnp.bfloat16),
            pltpu.VMEM((1, BLK // 2, HD), jnp.bfloat16),
            pltpu.SemaphoreType.DMA((3, SEGMENTS)),
        ],
        name="live_upper",
        mib=60,
    )


def live_rest(chain, cache_len, blocks):
    outs = ((BLK // 2, BLK, 0), (0, BLK // 2, HD), (BLK // 2, BLK, HD), (0, BLK, HD))
    shapes = [(CBLK, stop - start, HD) for start, stop, _ in outs]
    return chain(
        functools.partial(live_kernel, outs),
        (cache_len, blocks),
        [SM, HB],
        [HB] * len(outs),
        [pltpu.HBM(shape, jnp.bfloat16) for shape in shapes],
        [pltpu.VMEM(blocks.shape, jnp.bfloat16)]
        + [pltpu.VMEM(shape, jnp.bfloat16) for shape in shapes]
        + [pltpu.SemaphoreType.DMA((1 + len(outs), SEGMENTS))],
        name="live_rest",
        mib=32,
    )


def write_index(own_ref, table_ref, out_ref, note_ref):
    role = lax.axis_index("role")

    def column_rows(block):
        row = jnp.concatenate([block[0:1], block[1:2], block[2:3, : NBLK - 2 * HD]], axis=1)
        return jnp.broadcast_to(row, (8, NBLK))

    own_block = own_ref[...].astype(jnp.float32)
    sent_block = jnp.where(role == 0, own_block, table_ref[0].astype(jnp.float32))
    rows = jnp.concatenate([column_rows(own_block), column_rows(sent_block)], axis=0)
    tables = jnp.transpose(rows)
    own = tables[:, 0:1]
    sent = tables[:, 8:9]
    ids = lax.broadcasted_iota(jnp.int32, (NBLK, N_PIPE), 1).astype(jnp.float32)
    earlier = (
        lax.broadcasted_iota(jnp.int32, (NBLK, NBLK), 1)
        < lax.broadcasted_iota(jnp.int32, (NBLK, NBLK), 0)
    ).astype(jnp.bfloat16)

    def slots(column):
        onehot = column == ids
        before = jnp.dot(
            earlier, onehot.astype(jnp.bfloat16), preferred_element_type=jnp.float32
        )
        return jnp.sum(jnp.where(onehot, before, 0.0), axis=1, keepdims=True)

    own_slot = slots(own)
    sent_slot = slots(sent)
    turned = jnp.where(role == 0, jnp.where(sent >= 8.0, sent - 8.0, sent + 8.0), sent)
    slot_ids = lax.broadcasted_iota(jnp.int32, (1, SLOTS), 1)
    block = lax.broadcasted_iota(jnp.int32, (NBLK, 1), 0)

    def source(owner, slot):
        target = (owner * float(CAPB) + slot).astype(jnp.int32)
        return jnp.max(jnp.where(target == slot_ids, block, -1), axis=0, keepdims=True)

    sent_source = source(turned, sent_slot)
    out_ref[0:1, :] = jnp.where(sent_source < 0, NBLK, sent_source)
    own_source = source(own, own_slot)
    group = lax.div(slot_ids, CAPB)
    noted = slot_ids + group
    turned_ids = lax.rem(slot_ids + 8 * CAPB, SLOTS)
    turned_noted = lax.rem(noted + 8 * NOTED, N_PIPE * NOTED)
    own_noted = jnp.where(own_source < 0, N_PIPE * NOTED, own_source)
    out_ref[1:2, :] = jnp.where(role == 0, own_noted, turned_noted)
    out_ref[2:3, :] = jnp.where(role == 0, own_noted, noted)
    out_ref[3:4, :] = jnp.where(
        role == 0, jnp.where(own_source < 0, SLOTS, own_source), turned_ids
    )

    lanes = lax.broadcasted_iota(jnp.int32, (BLK, HD), 1)
    both = jnp.where(lanes == 0, sent_slot[CBLK:, :], sent[CBLK:, :])
    both = jnp.concatenate([both, jnp.full((HD - BLK, HD), -1.0, jnp.float32)], axis=0)
    both = jnp.transpose(both)
    for q in range(N_PIPE):
        note = jnp.where(both[1:2, :] == float(q), both[0:1, :], -1.0)
        note_ref[q] = jnp.broadcast_to(note, (BLK // 2, HD)).astype(jnp.bfloat16)


def fill_slots(index_ref, held, filled, out_ref, sems, note_ref=None):
    stride = CAPB if note_ref is None else NOTED
    for ref in held:
        ref[pl.ds(CBLK, BLK + 1)] = jnp.zeros((BLK + 1,) + ref.shape[1:], ref.dtype)
    groups = N_PIPE // SEGMENTS
    copies = []
    for k in range(SEGMENTS):

        def group_step(g, _):
            for s in range(CAPB):
                i = index_ref[0, g * CAPB + s]
                for j, ref in enumerate(held):
                    filled[g * stride + s, j * BLK // 2 : (j + 1) * BLK // 2] = ref[i]
            if note_ref is not None:
                filled[g * stride + CAPB] = note_ref[g]
            return 0

        lax.fori_loop(k * groups, (k + 1) * groups, group_step, 0)
        part = pl.ds(k * groups * stride, groups * stride)
        copies.append(pltpu.make_async_copy(filled.at[part], out_ref.at[part], sems.at[k]))
        copies[-1].start()
    for copy in copies:
        copy.wait()


def first_kernel(
    own_table, own_ref, crossed_ref, out_ref, index_ref, held, table, note, filled, listed, sems
):
    role = lax.axis_index("role")
    cached = pl.ds(0, CBLK)
    tables = pltpu.make_async_copy(
        crossed_ref.at[pl.ds(CBLK, 1)], table, sems.at[SEGMENTS + 1]
    )
    tables.start()

    @pl.when(role == 0)
    def _():
        pltpu.make_async_copy(own_ref, held.at[cached], sems.at[SEGMENTS]).start()

    @pl.when(role != 0)
    def _():
        pltpu.make_async_copy(
            crossed_ref.at[cached], held.at[cached], sems.at[SEGMENTS]
        ).start()

    tables.wait()
    write_index(own_table, table, index_ref, note)
    listing = pltpu.make_async_copy(index_ref, listed, sems.at[SEGMENTS + 2])
    listing.start()
    pltpu.make_async_copy(own_ref, held.at[cached], sems.at[SEGMENTS]).wait()
    listing.wait()
    fill_slots(listed, (held,), filled, out_ref, sems, note)


def first_dispatch(chain, table, own, crossed):
    half = (BLK // 2, HD)
    entries = N_PIPE * NOTED
    return chain(
        first_kernel,
        (table, own, crossed),
        [VM, HB, HB],
        [HB, VM],
        [pltpu.HBM((entries,) + half, jnp.bfloat16), like((4, SLOTS), jnp.int32)],
        [
            pltpu.VMEM((NBLK + 1,) + half, jnp.bfloat16),
            pltpu.VMEM((1,) + half, jnp.bfloat16),
            pltpu.VMEM((N_PIPE,) + half, jnp.bfloat16),
            pltpu.VMEM((entries,) + half, jnp.bfloat16),
            pltpu.SMEM((4, SLOTS), jnp.int32),
            pltpu.SemaphoreType.DMA((SEGMENTS + 3,)),
        ],
        name="first_dispatch",
        mib=24,
    )


def second_kernel(index_ref, *refs):
    own, crossed, out_ref, held, filled, sems = refs[:2], refs[2:4], refs[4], refs[5:7], *refs[7:]
    cached = pl.ds(0, CBLK)

    def load(sources):
        run_copies(
            [
                pltpu.make_async_copy(sources[j], held[j].at[cached], sems.at[SEGMENTS + j])
                for j in range(2)
            ]
        )

    @pl.when(lax.axis_index("role") == 0)
    def _():
        load(own)

    @pl.when(lax.axis_index("role") != 0)
    def _():
        load(crossed)

    fill_slots(index_ref, held, filled, out_ref, sems)


def second_dispatch(chain, index, own, crossed):
    return chain(
        second_kernel,
        (index, *own, *crossed),
        [SM] + [HB] * 4,
        [HB],
        [pltpu.HBM((SLOTS, BLK, HD), jnp.bfloat16)],
        [pltpu.VMEM((NBLK + 1, BLK // 2, HD), jnp.bfloat16)] * 2
        + [
            pltpu.VMEM((SLOTS, BLK, HD), jnp.bfloat16),
            pltpu.SemaphoreType.DMA((SEGMENTS + 2,)),
        ],
        name="second_dispatch",
        mib=24,
    )[0]


def place_kernel(index_ref, *refs):
    own, own_fresh, got = refs[0:3], refs[3:6], refs[6:9]
    near_ref, far_ref, out_ref = refs[9:12]
    held = refs[12:15]
    fresh, filled, notes, places, sems, out_sems = refs[15:]
    role = lax.axis_index("role")
    me = lax.axis_index("pipe")
    y = lax.div(me, 8)
    column = lax.rem(lax.div(me, 2), 4)
    core = lax.rem(me, 2)
    groups = N_PIPE // SEGMENTS
    for ref in held:
        ref[ref.shape[0] - 1] = jnp.zeros(ref.shape[1:], ref.dtype)

    def loads(k):
        copies = []
        for j in range(3):
            stride = CAPB if j == 2 else NOTED
            turn = k if j == 1 else (k + 2) % SEGMENTS
            part = pl.ds(turn * groups * stride, groups * stride)
            copies.append(
                pltpu.make_async_copy(got[j].at[part], held[j].at[part], sems.at[j, k])
            )
        return copies

    def fill(k):
        def group_step(g, _):
            for s in range(CAPB):
                r = g * CAPB + s
                filled[r, : BLK // 2, :HD] = held[0][index_ref[1, r]]
                filled[r, BLK // 2 :, :HD] = held[1][index_ref[2, r]]
                filled[r, :, HD:] = held[2][index_ref[3, r]]
            return 0

        lax.fori_loop(k * groups, (k + 1) * groups, group_step, 0)

    def store(k):
        part = pl.ds(k * groups * CAPB, groups * CAPB)
        return pltpu.make_async_copy(filled.at[part], out_ref.at[part], out_sems.at[k])

    @pl.when(role == 0)
    def _():
        copies = []
        for j in range(3):
            copies.append(
                pltpu.make_async_copy(
                    own[j].at[pl.ds(0, CBLK)], held[j].at[pl.ds(0, CBLK)], sems.at[j, 0]
                )
            )
            copies.append(
                pltpu.make_async_copy(
                    own_fresh[j], held[j].at[pl.ds(CBLK, BLK)], sems.at[j, 1]
                )
            )
        run_copies(copies)
        for k in range(SEGMENTS):
            fill(k)
            store(k).start()
        for k in range(SEGMENTS):
            store(k).wait()

    def patch(k):
        def one(p, _):
            sender = jnp.where(lax.div(p, 8) == y, 1, 0)
            back = lax.rem(column - lax.rem(lax.div(p, 2), 4) + 7 + sender, 4)
            second = jnp.where(lax.rem(p, 2) == sender, 0, 1)
            side = jnp.where(sender == core, 0, 1)
            row = ((side * 4 + back) * 2 + second) * BLK
            for j in range(BLK):
                filled[places[p, j]] = fresh[row + j]
            return 0

        lax.fori_loop(k * groups, (k + 1) * groups, one, 0)

    @pl.when(role != 0)
    def _():
        arrivals = [loads(k) for k in range(SEGMENTS)]
        moves = [
            pltpu.make_async_copy(
                ref, fresh.at[pl.ds(side * 8 * BLK, 8 * BLK)], sems.at[3, side]
            )
            for side, ref in enumerate((near_ref, far_ref))
        ]
        for k in range(SEGMENTS):
            arrivals[k][0].start()
        for copy in moves:
            copy.start()
        for k in range(SEGMENTS):
            arrivals[k][1].start()
            arrivals[k][2].start()
        for k in range(SEGMENTS):
            arrivals[k][0].wait()
        for i in range(N_PIPE):
            p = (i + 8) % N_PIPE
            slot = held[0][i * NOTED + CAPB][0:1, :].astype(jnp.float32)
            spot = jnp.where(slot >= 0.0, slot + float(p * CAPB), float(SLOTS))
            notes[p : p + 1, :] = spot.astype(jnp.int32)
        listing = pltpu.make_async_copy(notes, places, out_sems.at[SEGMENTS])
        listing.start()
        for k in range(SEGMENTS):
            arrivals[k][1].wait()
            arrivals[k][2].wait()
            fill(k)
            if k == 0:
                listing.wait()
                for copy in moves:
                    copy.wait()
            patch(k)
            store(k).start()
        for k in range(SEGMENTS):
            store(k).wait()


def place(chain, index, own, own_fresh, got, near, far):
    entries = N_PIPE * NOTED
    return chain(
        place_kernel,
        (index, *own, *own_fresh, *got, near, far),
        [SM] + [HB] * 3 + [VM] * 3 + [HB] * 5,
        [HB],
        [pltpu.HBM((SLOTS, BLK, 2 * HD), jnp.bfloat16)],
        [
            pltpu.VMEM((entries + 1, BLK // 2, HD), jnp.bfloat16),
            pltpu.VMEM((entries + 1, BLK // 2, HD), jnp.bfloat16),
            pltpu.VMEM((SLOTS + 1, BLK, HD), jnp.bfloat16),
            pltpu.VMEM((N_PIPE * BLK, BLK, 2 * HD), jnp.bfloat16),
            pltpu.VMEM((SLOTS + 1, BLK, 2 * HD), jnp.bfloat16),
            pltpu.VMEM((N_PIPE, HD), jnp.int32),
            pltpu.SMEM((N_PIPE, HD), jnp.int32),
            pltpu.SemaphoreType.DMA((4, SEGMENTS)),
            pltpu.SemaphoreType.DMA((SEGMENTS + 1,)),
        ],
        name="place",
        mib=60,
    )[0]


TOTAL = CAP + ROWS
CHUNKS = tuple((k, 512) for k in range(0, CAP, 512)) + ((CAP, ROWS),)


def attend_kernel(start, heads, q_ref, kv_ref, fresh_ref, len_ref, *refs):
    out_ref, bias, keys, values, first, second, mixed, sem = refs[-8:]
    keys[:CAP, :] = kv_ref[:, :HD]
    keys[CAP:, :] = fresh_ref[:, :, :HD].reshape(ROWS, HD)
    values[:CAP, :HD] = kv_ref[:, HD:]
    values[CAP:, :HD] = fresh_ref[:, :, HD:].reshape(ROWS, HD)
    values[:, HD:] = jnp.ones((TOTAL, HD), jnp.bfloat16)
    lengths = jnp.transpose(jnp.broadcast_to(len_ref[...].astype(jnp.float32), (HD, ROWS)))
    ids = lax.broadcasted_iota(jnp.int32, (ROWS, HD), 1).astype(jnp.float32)
    for k in range(0, CAP, HD):
        bias[:, k : k + HD] = jnp.where(ids + float(k) < lengths, 0.0, NEG_FILL)
    row = lax.broadcasted_iota(jnp.int32, (ROWS, ROWS), 0)
    column = lax.broadcasted_iota(jnp.int32, (ROWS, ROWS), 1)
    prefill = lax.axis_index("role") == 0
    bias[:, CAP:] = jnp.where(
        jnp.logical_and(column <= row, jnp.logical_or(prefill, column == row)), 0.0, NEG_FILL
    )
    held = (first, second)

    def score(head, k, size, top):
        part = lax.dot_general(
            q_ref[:, (start + head) * HD : (start + head + 1) * HD],
            keys[k : k + size, :],
            (((1,), (1,)), ((), ())),
            preferred_element_type=jnp.float32,
        )
        part = part + bias[:, k : k + size]
        held[head % 2][:, k : k + size] = part
        for j in range(0, size, HD):
            top = jnp.maximum(top, part[:, j : j + HD])
        return top

    def mix(head, k, size, top, total):
        weights = jnp.exp2((held[head % 2][:, k : k + size] - top) * EXP_SCALE)
        return total + jnp.dot(
            weights.astype(jnp.bfloat16),
            values[k : k + size, :],
            preferred_element_type=jnp.float32,
        )

    best = None
    for head in range(heads + 1):
        top = jnp.full((ROWS, HD), NEG_FILL, jnp.float32)
        total = jnp.zeros((ROWS, 2 * HD), jnp.float32)
        for k, size in CHUNKS:
            if head < heads:
                top = score(head, k, size, top)
            if head > 0:
                total = mix(head - 1, k, size, best, total)
        if head > 0:
            mixed[:, (head - 1) * HD : head * HD] = (
                total[:, :HD] / total[:, HD:]
            ).astype(jnp.bfloat16)
        if head < heads:
            best = jnp.max(top, axis=1, keepdims=True)
    columns = pl.ds(start * HD, heads * HD)
    run_copies([pltpu.make_async_copy(mixed, out_ref.at[:, columns], sem)])


def attend(chain, queries, cache, fresh, cache_len, start, heads, others=()):
    return chain(
        functools.partial(attend_kernel, start, heads),
        (queries, cache, fresh, cache_len, *others),
        [VM] * 4 + [HB] * len(others),
        [HB],
        [pltpu.HBM((ROWS, GROUP * HD), jnp.bfloat16)],
        [
            pltpu.VMEM((ROWS, TOTAL), jnp.float32),
            pltpu.VMEM((TOTAL, HD), jnp.bfloat16),
            pltpu.VMEM((TOTAL, 2 * HD), jnp.bfloat16),
            pltpu.VMEM((ROWS, TOTAL), jnp.float32),
            pltpu.VMEM((ROWS, TOTAL), jnp.float32),
            pltpu.VMEM((ROWS, heads * HD), jnp.bfloat16),
            pltpu.SemaphoreType.DMA,
        ],
        name="attend",
        mib=40,
        aliases={4: 0} if others else None,
    )[0]


def rotation(lengths):
    row_ids = jnp.arange(ROWS, dtype=jnp.int32)
    positions = lengths + jnp.where(lax.axis_index("role") == 0, row_ids, 0)
    frequency = ROPE_BASE ** (-2.0 * jnp.arange(HD // 2, dtype=jnp.float32) / HD)
    angles = positions.astype(jnp.float32)[:, None] * frequency[None, :]
    cosine, sine = jnp.cos(angles), jnp.sin(angles)
    return jnp.concatenate([cosine, cosine], axis=1), jnp.concatenate([-sine, sine], axis=1)


def local(hidden, norm_gain, kv_weight, queries, kv_cache, cache_len, block_table):
    chain = Chain()
    cache = kv_cache[0]
    query_rows = queries[0]
    blocks = cache.reshape(CBLK, BLK, 2 * HD)
    cosine, sine = rotation(cache_len[0])

    upper, table = live_upper(chain, cache_len, blocks, block_table)
    upper_crossed = cross(upper)
    lower, value_upper, value_lower, value = live_rest(chain, cache_len, blocks)
    halves = value_upper, value_lower
    halves_crossed = cross(value_upper), cross(value_lower)
    high, low, *sums = project(chain, hidden[0], norm_gain[None], kv_weight)

    def early(operands):
        table, lower, crossed, high, low, sums, chain.token = operands
        sent, index = first_dispatch(chain, table, lower, crossed)
        got = pipe_exchange(sent)
        high, low = ring_shift(high, low)
        for k in range(2):
            high, low = ring_shift(*add_step(chain, high, low, sums[2 * k], sums[2 * k + 1]))
        return index, got, high, low, chain.token

    operands = (table, lower, upper_crossed, high, low, sums[:4], chain.token)
    index, got_upper, high, low, chain.token = fenced(early, operands)
    sent_value = second_dispatch(chain, index, halves, halves_crossed)
    got_value = pipe_exchange(sent_value)

    def late(operands):
        high, low, sums, cosine, sine, chain.token = operands
        high, low = ring_shift(*add_step(chain, high, low, sums[0], sums[1]))
        fresh, *own_fresh = fresh_rows(chain, sums[2], high, low, cosine, sine)
        moved, beside = cross(fresh), cross(fresh, 9)
        attention = attend(chain, query_rows, cache, fresh, cache_len, 0, 2)
        return attention, fresh, own_fresh, moved, beside, chain.token

    got_lower = cross(got_upper)
    operands = (high, low, sums[4:], cosine, sine, chain.token)
    attention, fresh, own_fresh, moved, beside, chain.token = fenced(late, operands)
    pair, got_lower = pack(chain, (moved, beside), (got_lower,))
    reached = [spread(pair, k) for k in range(4)]
    attention = attend(chain, query_rows, cache, fresh, cache_len, 2, 4, (attention,))
    (near,) = pack(chain, reached, (), pair)
    far = pipe_move(near, lambda y, c, core: (y, c, 1 - core))
    attention = attend(chain, query_rows, cache, fresh, cache_len, 6, 2, (attention,))
    received = place(
        chain,
        index,
        (upper, lower, value),
        own_fresh,
        (got_upper, got_lower, got_value),
        near,
        far,
    )
    return (attention[None], received.reshape(1, SLOTS * BLK, 2 * HD))


def solution(mesh):
    in_specs = (
        P("role", "pipe", "tp"),
        P("tp"),
        P("tp", None),
        P("role", "pipe", "tp"),
        P("role", "pipe", "tp"),
        P("role", "pipe"),
        P("pipe"),
    )
    out_specs = (P("role", "pipe", "tp"), P("role", "pipe", "tp"))
    return jax.shard_map(local, mesh=mesh, in_specs=in_specs, out_specs=out_specs, check_vma=False)
```
